32 devices in a mesh: groups: 2 (over y), hid: 4 (over x, core), wid: 4 (over z).
Axes of the slice: x: 2, y: 2, z: 4, core: 2. Of those that a mesh axis runs over, the one named last changes fastest.
Arguments:
- tokens: bfloat16 [2048, 6144], P(('groups', 'wid'), 'hid'), parts along dimension 0, may hold values from -6 to 6
- ln_gain: bfloat16 [6144], P('hid'), may hold values from 0.5 to 2
- w_query: bfloat16 [6144, 6144], P('hid', 'wid'), may hold values from -1 to 1
- w_key: bfloat16 [6144, 6144], P('hid', 'wid'), may hold values from -1 to 1
- w_value: bfloat16 [6144, 6144], P('hid', 'wid'), may hold values from -0.078125 to 0.078125
- w_in: bfloat16 [6144, 24576], P('hid', 'wid'), may hold values from -0.078125 to 0.078125
- query_gain: float32 [6144], P('wid'), may hold values from 0.5 to 5
- key_gain: float32 [6144], P('wid'), may hold values from 0.5 to 5
- w_attn_out: bfloat16 [6144, 6144], P('wid', 'hid'), may hold values from -0.5 to 0.5
- w_mlp_out: bfloat16 [24576, 6144], P('wid', 'hid'), may hold values from -0.0390625 to 0.0390625
Outputs:
- layer_out: bfloat16 [2048, 6144], P(('groups', 'wid'), 'hid'), parts along dimension 0
The draws below stay inside these ranges and needn't reach their ends.
There are 2 independent parts, one for each index of `groups`. The reference program is written for one: setup_inputs(seed, part) draws one part's arguments, and reference() takes and returns one part's arrays. A program takes and returns all parts, laid end to end along the dimension named above; an argument that names none is the same for every part. Nothing has to cross between parts.
All inputs are finite; a program needn't handle non-finite values.
Results may differ from the reference program's by a relative error of at most 0.012.
The reference program's roundings to bfloat16 on the way (of `normed`, `probs`, `attended` and `act`) count: a program that leaves them out, or rounds other values in their place, can miss the bound.
Values may be sent and summed in bfloat16 or wider, within the bound.
A program may use at most 256 MiB of HBM per device.

```python
import math
import jax
import jax.numpy as jnp
from jax import lax

D = 6144
FF = 24576
HEAD = 128
PATCHES = 256
IMAGES = 4
TOKENS = 1024


def shared_weight(key):
    base = jax.random.truncated_normal(jax.random.fold_in(key, 2000), -6.0, 6.0, (D, D), jnp.float32)
    return base * D ** (-0.5)


def gain_values(key, low, high):
    return jax.random.uniform(key, (D,), jnp.float32, low, high)


def draw_tokens(key, part):
    key = jax.random.fold_in(key, 7)
    base = jax.random.truncated_normal(key, -6.0, 6.0, (TOKENS, D), jnp.float32)
    return base.astype(jnp.bfloat16)


def draw_w_query(key, part):
    return shared_weight(key).astype(jnp.bfloat16)


def draw_w_key(key, part):
    key = jax.random.fold_in(key, 37)
    own = jax.random.truncated_normal(key, -6.0, 6.0, (D, D), jnp.float32) * D ** (-0.5)
    return own.astype(jnp.bfloat16)


def draw_query_gain(key, part):
    key = jax.random.fold_in(key, 11)
    return jnp.exp(gain_values(key, jnp.log(0.5), jnp.log(5.0)))


def draw_key_gain(key, part):
    key = jax.random.fold_in(key, 23)
    return jnp.exp(gain_values(key, jnp.log(0.5), jnp.log(5.0)))


def block_levels(stream_key, shape, shards, least, high):
    factor_of = 1.0
    for position, parts in shards:
        steps = jax.random.uniform(jax.random.fold_in(jax.random.fold_in(stream_key, 6), position), (parts,), jnp.float32, least / len(shards), high / len(shards))
        factor_of = factor_of * jnp.repeat(jnp.exp(steps), shape[position] // parts).reshape((-1,) + (1,) * (len(shape) - 1 - position))
    return factor_of


def normal_values(key, shape, scale, limit, shards=(), held_as=jnp.bfloat16):
    drawn = jax.random.normal(key, shape, jnp.float32) * scale
    if len(shards) > 0:
        drawn = block_levels(key, shape, shards, -0.22, 0.18) * drawn
    return jnp.clip(drawn, min=-limit, max=limit).astype(held_as)


def setup_inputs(seed: int = 0, part: int = 0) -> dict:
    splits = jax.random.split(jax.random.key(seed), 11)
    part_splits = jax.random.split(jax.random.fold_in(splits[10], part), 11)
    return {
        "tokens": draw_tokens(jax.random.fold_in(jax.random.fold_in(splits[10], part), 71), part),
        "ln_gain": jnp.clip(jnp.exp(math.log(2.0) - 1.3862944 * jax.random.uniform(splits[1], (D,), jnp.float32) ** block_levels(splits[1], (D,), ((0, 4),), -0.2, 0.2)), 0.5, 2.0).astype(jnp.bfloat16),
        "w_query": draw_w_query(jax.random.fold_in(splits[10], 71), part),
        "w_key": draw_w_key(jax.random.fold_in(splits[10], 71), part),
        "w_value": normal_values(splits[4], (D, D), D ** -0.5, 0.078125, ((0, 4), (1, 4))),
        "w_in": normal_values(splits[5], (D, FF), D ** -0.5, 0.078125, ((0, 4), (1, 4))),
        "query_gain": draw_query_gain(jax.random.fold_in(splits[10], 71), part),
        "key_gain": draw_key_gain(jax.random.fold_in(splits[10], 71), part),
        "w_attn_out": normal_values(splits[8], (D, D), HEAD ** -0.5, 0.5, ((0, 4), (1, 4))),
        "w_mlp_out": normal_values(splits[9], (FF, D), FF ** -0.5, 0.0390625, ((0, 4), (1, 4))),
    }


def norm_rows(values, gain):
    mean = lax.optimization_barrier(jnp.mean(values, axis=-1, keepdims=True))
    square = lax.optimization_barrier(jnp.mean(values * values, axis=-1, keepdims=True))
    return (values - mean) * lax.rsqrt(square - mean * mean + 1e-06) * gain

def head_norm(values, gain):
    rows = values.shape[0]
    shaped = values.reshape(rows, -1, HEAD)
    return norm_rows(shaped, gain.reshape(-1, HEAD)).reshape(rows, -1)

def reference(tokens, ln_gain, w_query, w_key, w_value, w_in, query_gain, key_gain, w_attn_out, w_mlp_out):
    tokens_f = tokens.astype(jnp.float32)
    normed = norm_rows(tokens_f, ln_gain.astype(jnp.float32)).astype(jnp.bfloat16)
    query = jnp.dot(normed, w_query, preferred_element_type=jnp.float32)
    key = jnp.dot(normed, w_key, preferred_element_type=jnp.float32)
    value = jnp.dot(normed, w_value, preferred_element_type=jnp.float32)
    pre = jnp.dot(normed, w_in, preferred_element_type=jnp.float32)
    queries = head_norm(query, query_gain).astype(jnp.bfloat16)
    keys = head_norm(key, key_gain).astype(jnp.bfloat16)
    values = value.astype(jnp.bfloat16)
    shape4 = (IMAGES, PATCHES, D // HEAD, HEAD)
    q4 = queries.reshape(shape4).astype(jnp.float32)
    k4 = keys.reshape(shape4).astype(jnp.float32)
    v4 = values.reshape(shape4).astype(jnp.float32)
    scores = jnp.einsum('iqhd,ikhd->ihqk', q4, k4) / jnp.sqrt(jnp.float32(HEAD))
    top = lax.optimization_barrier(jnp.max(scores, axis=-1, keepdims=True))
    expd = jnp.exp(scores - top)
    probs = (expd / lax.optimization_barrier(jnp.sum(expd, axis=-1, keepdims=True))).astype(jnp.bfloat16)
    attended = jnp.einsum('ihqk,ikhd->iqhd', probs.astype(jnp.float32), v4)
    attended = attended.astype(jnp.bfloat16).reshape(TOKENS, D)
    act = jax.nn.gelu(pre, approximate=False).astype(jnp.bfloat16)
    total = jnp.dot(attended, w_attn_out, preferred_element_type=jnp.float32)
    total = total + jnp.dot(act, w_mlp_out, preferred_element_type=jnp.float32)
    return (tokens_f + total).astype(jnp.bfloat16)
```

```python
import jax
import jax.numpy as jnp
from jax import lax
from jax.sharding import PartitionSpec as P

HEAD = 128
PATCHES = 256
QK_FAR = jnp.bfloat16


def head_norm(values, gain):
    rows = values.shape[0]
    shaped = values.reshape(rows, -1, HEAD)
    mean = jnp.mean(shaped, axis=-1, keepdims=True)
    square = jnp.mean(shaped * shaped, axis=-1, keepdims=True)
    normed = (shaped - mean) * lax.rsqrt(square - mean * mean + 1e-06) * gain.reshape(-1, HEAD)
    return normed.reshape(rows, -1)


def position_major(values):
    images = values.shape[0] // PATCHES
    shaped = values.reshape(images, PATCHES, values.shape[1])
    return jnp.transpose(shaped, (1, 0, 2)).reshape(values.shape)


def image_major(values):
    images = values.shape[0] // PATCHES
    shaped = values.reshape(PATCHES, images, values.shape[1])
    return jnp.transpose(shaped, (1, 0, 2)).reshape(values.shape)


def per_device(
    tokens, ln_gain, w_query, w_key, w_value, w_in, query_gain, key_gain, w_attn_out, w_mlp_out
):
    n_hid = lax.axis_size("hid")
    tokens_f = tokens.astype(jnp.float32)
    local_width = tokens.shape[1]
    width = local_width * n_hid
    first, second = lax.psum(
        (jnp.sum(tokens_f, axis=1), jnp.sum(tokens_f * tokens_f, axis=1)), "hid"
    )
    mean = first[:, None] / width
    square = second[:, None] / width
    normed = (
        (tokens_f - mean) * lax.rsqrt(square - mean * mean + 1e-06) * ln_gain.astype(jnp.float32)
    ).astype(jnp.bfloat16)
    gathered = lax.all_gather(normed, "wid", axis=0, tiled=True)
    normed_all = position_major(gathered)
    images = normed_all.shape[0] // PATCHES
    query_rows = normed_all.shape[0] // n_hid
    columns = w_query.shape[1]
    summed = lax.psum_scatter(
        jnp.concatenate(
            [
                jnp.dot(normed_all, weight, preferred_element_type=jnp.float32)
                for weight in (w_query, w_in)
            ],
            axis=1,
        ),
        "hid",
        scatter_dimension=0,
        tiled=True,
    )
    query = summed[:, :columns]
    pre = summed[:, columns:]
    key_sum, value_sum = lax.psum(
        (
            jnp.dot(normed_all, w_key, preferred_element_type=jnp.float32),
            jnp.dot(normed_all, w_value, preferred_element_type=jnp.float32),
        ),
        "hid",
    )
    keys_all = head_norm(key_sum, key_gain).astype(jnp.bfloat16)
    values_all = value_sum.astype(jnp.bfloat16)
    queries = head_norm(query, query_gain).astype(jnp.bfloat16)
    heads_local = columns // HEAD
    positions = query_rows // images
    keys_grid = keys_all.reshape(PATCHES, images, heads_local, HEAD)
    values_grid = values_all.reshape(PATCHES, images, heads_local, HEAD)
    query_grid = queries.reshape(positions, images, heads_local, HEAD)
    scores = jnp.einsum(
        "qihd,kihd->ihqk", query_grid, keys_grid, preferred_element_type=jnp.float32
    ) / jnp.sqrt(jnp.float32(HEAD))
    top = jnp.max(scores, axis=-1, keepdims=True)
    expd = jnp.exp(scores - top)
    probs = (expd / jnp.sum(expd, axis=-1, keepdims=True)).astype(jnp.bfloat16)
    attended = jnp.einsum("ihqk,kihd->qihd", probs, values_grid, preferred_element_type=jnp.float32)
    attended = attended.astype(jnp.bfloat16).reshape(query_rows, columns)
    act = jax.nn.gelu(pre, approximate=False).astype(jnp.bfloat16)
    joined = jnp.concatenate([attended, act], axis=1)
    piece = lax.all_gather(joined, "hid", axis=0, tiled=True)
    total = jnp.dot(piece[:, :columns], w_attn_out, preferred_element_type=jnp.float32)
    partial_out = image_major(
        total + jnp.dot(piece[:, columns:], w_mlp_out, preferred_element_type=jnp.float32)
    )
    total = lax.psum_scatter(partial_out, "wid", scatter_dimension=0, tiled=True)
    return (tokens_f + total).astype(jnp.bfloat16)


def fast_fits(tokens, w_query):
    n_hid, n_wid = lax.axis_size("hid"), lax.axis_size("wid")
    heads = w_query.shape[1] // HEAD
    return n_hid == 4 and n_wid > 1 and tokens.shape[0] % PATCHES == 0 and heads % n_hid == 0


def swap(values, bit):
    return lax.ppermute(values, "hid", [(i, i ^ bit) for i in range(lax.axis_size("hid"))])


def onward(values):
    n = lax.axis_size("wid")
    return lax.ppermute(values, "wid", [(i, (i + 1) % n) for i in range(n)])


def pick(values, index, quarter, side):
    first, second = values[:, : 2 * quarter], values[:, 2 * quarter :]
    if side:
        return jnp.where(index == 0, first, second)
    low = jnp.concatenate([first[:, :quarter], second[:, :quarter]], axis=1)
    high = jnp.concatenate([first[:, quarter:], second[:, quarter:]], axis=1)
    return jnp.where(index == 0, low, high)


def half(values, index):
    width = values.shape[1] // 2
    return jnp.where(index == 0, values[:, :width], values[:, width:])


def reduce_columns(values, core, side, near, far):
    quarter = values.shape[1] // 4
    sent = swap(pick(values, 1 - core, quarter, False).astype(near), 1)
    paired = pick(values, core, quarter, False) + sent.astype(jnp.float32)
    other = swap(half(paired, 1 - side).astype(far), 2)
    return half(paired, side) + other.astype(jnp.float32)


def gather_columns(own, core, side):
    across = swap(own, 2)
    own_near = swap(own, 1)
    across_near = swap(across, 1)
    here = [jnp.where(core == 0, own, own_near), jnp.where(core == 0, own_near, own)]
    there = [jnp.where(core == 0, across, across_near), jnp.where(core == 0, across_near, across)]
    return jnp.concatenate(
        [jnp.where(side == 0, a, b) for a, b in zip(here + there, there + here)], axis=1
    )


def attend(query, key, value, query_gain, key_gain):
    rows, columns = query.shape
    images = rows // PATCHES
    grid = (images, PATCHES, columns // HEAD, HEAD)
    queries = head_norm(query, query_gain).astype(jnp.bfloat16).reshape(grid)
    keys = head_norm(key, key_gain).astype(jnp.bfloat16).reshape(grid)
    values = value.astype(jnp.bfloat16).reshape(grid)
    scores = jnp.einsum(
        "iqhd,ikhd->ihqk", queries, keys, preferred_element_type=jnp.float32
    ) / jnp.sqrt(jnp.float32(HEAD))
    top = jnp.max(scores, axis=-1, keepdims=True)
    expd = jnp.exp(scores - top)
    probs = (expd / jnp.sum(expd, axis=-1, keepdims=True)).astype(jnp.bfloat16)
    attended = jnp.einsum("ihqk,ikhd->iqhd", probs, values, preferred_element_type=jnp.float32)
    return attended.astype(jnp.bfloat16).reshape(rows, columns)


def ringed(
    tokens, ln_gain, w_query, w_key, w_value, w_in, query_gain, key_gain, w_attn_out, w_mlp_out
):
    n_hid, n_wid = lax.axis_size("hid"), lax.axis_size("wid")
    hid = lax.axis_index("hid")
    core, side = hid % 2, hid // 2
    width = tokens.shape[1] * n_hid
    quarter = w_query.shape[1] // n_hid
    tokens_f = tokens.astype(jnp.float32)
    sums = jnp.stack([jnp.sum(tokens_f, axis=1), jnp.sum(tokens_f * tokens_f, axis=1)])
    sums = sums + swap(sums, 1)
    sums = sums + swap(sums, 2)
    mean = sums[0][:, None] / width
    square = sums[1][:, None] / width
    block = (
        (tokens_f - mean) * lax.rsqrt(square - mean * mean + 1e-06) * ln_gain.astype(jnp.float32)
    ).astype(jnp.bfloat16)
    my_query_gain = lax.dynamic_slice_in_dim(query_gain, hid * quarter, quarter)
    my_key_gain = lax.dynamic_slice_in_dim(key_gain, hid * quarter, quarter)
    blocks = [block]
    for _ in range(n_wid - 1):
        blocks.append(onward(blocks[-1]))
    running = None
    for block in blocks:
        query, key, value, pre = [
            jnp.dot(block, weight, preferred_element_type=jnp.float32)
            for weight in (w_query, w_key, w_value, w_in)
        ]
        query = reduce_columns(query, core, side, jnp.float32, QK_FAR)
        key = reduce_columns(key, core, side, jnp.float32, QK_FAR)
        value = reduce_columns(value, core, side, jnp.bfloat16, jnp.bfloat16)
        pre = reduce_columns(pre, core, side, jnp.bfloat16, jnp.bfloat16)
        act = jax.nn.gelu(pre, approximate=False).astype(jnp.bfloat16)
        act = gather_columns(act, core, side)
        attended = attend(query, key, value, my_query_gain, my_key_gain)
        attended = gather_columns(attended, core, side)
        total = jnp.dot(act, w_mlp_out, preferred_element_type=jnp.float32)
        total = total + jnp.dot(attended, w_attn_out, preferred_element_type=jnp.float32)
        if running is not None:
            total = total + running.astype(jnp.float32)
        running = onward(total.astype(jnp.bfloat16))
    return (tokens_f + running.astype(jnp.float32)).astype(jnp.bfloat16)


def choose(*args):
    if fast_fits(args[0], args[2]):
        return ringed(*args)
    return per_device(*args)


def solution(mesh):
    in_specs = (
        P(("groups", "wid"), "hid"),
        P("hid"),
        P("hid", "wid"),
        P("hid", "wid"),
        P("hid", "wid"),
        P("hid", "wid"),
        P("wid"),
        P("wid"),
        P("wid", "hid"),
        P("wid", "hid"),
    )
    out_specs = P(("groups", "wid"), "hid")
    return jax.shard_map(
        choose, mesh=mesh, in_specs=in_specs, out_specs=out_specs, check_vma=False
    )
```

```python
import jax
import jax.numpy as jnp
from jax import lax
from jax.experimental import pallas as pl
from jax.experimental.pallas import tpu as pltpu
from jax.sharding import PartitionSpec as P

HEAD = 128
PATCHES = 256


def head_norm(values, gain):
    rows = values.shape[0]
    shaped = values.reshape(rows, -1, HEAD)
    mean = jnp.mean(shaped, axis=-1, keepdims=True)
    square = jnp.mean(shaped * shaped, axis=-1, keepdims=True)
    normed = (shaped - mean) * lax.rsqrt(square - mean * mean + 1e-06) * gain.reshape(-1, HEAD)
    return normed.reshape(rows, -1)


def position_major(values):
    images = values.shape[0] // PATCHES
    shaped = values.reshape(images, PATCHES, values.shape[1])
    return jnp.transpose(shaped, (1, 0, 2)).reshape(values.shape)


def image_major(values):
    images = values.shape[0] // PATCHES
    shaped = values.reshape(PATCHES, images, values.shape[1])
    return jnp.transpose(shaped, (1, 0, 2)).reshape(values.shape)


def per_device(
    tokens, ln_gain, w_query, w_key, w_value, w_in, query_gain, key_gain, w_attn_out, w_mlp_out
):
    n_hid = lax.axis_size("hid")
    tokens_f = tokens.astype(jnp.float32)
    local_width = tokens.shape[1]
    width = local_width * n_hid
    first, second = lax.psum(
        (jnp.sum(tokens_f, axis=1), jnp.sum(tokens_f * tokens_f, axis=1)), "hid"
    )
    mean = first[:, None] / width
    square = second[:, None] / width
    normed = (
        (tokens_f - mean) * lax.rsqrt(square - mean * mean + 1e-06) * ln_gain.astype(jnp.float32)
    ).astype(jnp.bfloat16)
    gathered = lax.all_gather(normed, "wid", axis=0, tiled=True)
    normed_all = position_major(gathered)
    images = normed_all.shape[0] // PATCHES
    query_rows = normed_all.shape[0] // n_hid
    columns = w_query.shape[1]
    summed = lax.psum_scatter(
        jnp.concatenate(
            [
                jnp.dot(normed_all, weight, preferred_element_type=jnp.float32)
                for weight in (w_query, w_in)
            ],
            axis=1,
        ),
        "hid",
        scatter_dimension=0,
        tiled=True,
    )
    query = summed[:, :columns]
    pre = summed[:, columns:]
    key_sum, value_sum = lax.psum(
        (
            jnp.dot(normed_all, w_key, preferred_element_type=jnp.float32),
            jnp.dot(normed_all, w_value, preferred_element_type=jnp.float32),
        ),
        "hid",
    )
    keys_all = head_norm(key_sum, key_gain).astype(jnp.bfloat16)
    values_all = value_sum.astype(jnp.bfloat16)
    queries = head_norm(query, query_gain).astype(jnp.bfloat16)
    heads_local = columns // HEAD
    positions = query_rows // images
    keys_grid = keys_all.reshape(PATCHES, images, heads_local, HEAD)
    values_grid = values_all.reshape(PATCHES, images, heads_local, HEAD)
    query_grid = queries.reshape(positions, images, heads_local, HEAD)
    scores = jnp.einsum(
        "qihd,kihd->ihqk", query_grid, keys_grid, preferred_element_type=jnp.float32
    ) / jnp.sqrt(jnp.float32(HEAD))
    top = jnp.max(scores, axis=-1, keepdims=True)
    expd = jnp.exp(scores - top)
    probs = (expd / jnp.sum(expd, axis=-1, keepdims=True)).astype(jnp.bfloat16)
    attended = jnp.einsum("ihqk,kihd->qihd", probs, values_grid, preferred_element_type=jnp.float32)
    attended = attended.astype(jnp.bfloat16).reshape(query_rows, columns)
    act = jax.nn.gelu(pre, approximate=False).astype(jnp.bfloat16)
    joined = jnp.concatenate([attended, act], axis=1)
    piece = lax.all_gather(joined, "hid", axis=0, tiled=True)
    total = jnp.dot(piece[:, :columns], w_attn_out, preferred_element_type=jnp.float32)
    partial_out = image_major(
        total + jnp.dot(piece[:, columns:], w_mlp_out, preferred_element_type=jnp.float32)
    )
    total = lax.psum_scatter(partial_out, "wid", scatter_dimension=0, tiled=True)
    return (tokens_f + total).astype(jnp.bfloat16)


def fast_fits(tokens, w_query):
    n_hid, n_wid = lax.axis_size("hid"), lax.axis_size("wid")
    heads = w_query.shape[1] // HEAD
    return n_hid == 4 and n_wid > 1 and tokens.shape[0] % PATCHES == 0 and heads % n_hid == 0


def swap(values, bit):
    return lax.ppermute(values, "hid", [(i, i ^ bit) for i in range(lax.axis_size("hid"))])


def onward(values):
    n = lax.axis_size("wid")
    return lax.ppermute(values, "wid", [(i, (i + 1) % n) for i in range(n)])


def pick(values, index, quarter, side):
    first, second = values[:, : 2 * quarter], values[:, 2 * quarter :]
    if side:
        return jnp.where(index == 0, first, second)
    low = jnp.concatenate([first[:, :quarter], second[:, :quarter]], axis=1)
    high = jnp.concatenate([first[:, quarter:], second[:, quarter:]], axis=1)
    return jnp.where(index == 0, low, high)


def half(values, index):
    width = values.shape[1] // 2
    return jnp.where(index == 0, values[:, :width], values[:, width:])


def reduce_columns(parts, core, side, near, far):
    quarters = [part.shape[1] // 4 for part in parts]
    sent = [pick(p, 1 - core, q, False).astype(near) for p, q in zip(parts, quarters)]
    sent = swap(jnp.concatenate(sent, axis=1), 1)
    paired, start = [], 0
    for part, quarter in zip(parts, quarters):
        got = sent[:, start : start + 2 * quarter].astype(jnp.float32)
        paired.append(pick(part, core, quarter, False) + got)
        start += 2 * quarter
    other = jnp.concatenate([half(p, 1 - side).astype(far) for p in paired], axis=1)
    return paired, swap(other, 2)


def gather_columns(own, core, side):
    across = swap(own, 2)
    own_near = swap(own, 1)
    across_near = swap(across, 1)
    here = [jnp.where(core == 0, own, own_near), jnp.where(core == 0, own_near, own)]
    there = [jnp.where(core == 0, across, across_near), jnp.where(core == 0, across_near, across)]
    return jnp.concatenate(
        [jnp.where(side == 0, a, b) for a, b in zip(here + there, there + here)], axis=1
    )


def attend_kernel(q_ref, k_ref, v_ref, other_ref, qg_ref, kg_ref, out_ref):
    width = out_ref.shape[1]
    hid = lax.axis_index("hid")
    side = hid // 2

    def total(ref, which, head):
        start = pl.multiple_of(side * width + head * HEAD, HEAD)
        column = which * width + head * HEAD
        return ref[:, pl.ds(start, HEAD)] + other_ref[:, column : column + HEAD].astype(jnp.float32)

    def unit(values, gain_ref, head):
        mean = jnp.mean(values, axis=1, keepdims=True)
        square = jnp.mean(values * values, axis=1, keepdims=True)
        gain = gain_ref[:, pl.ds(pl.multiple_of(hid * width + head * HEAD, HEAD), HEAD)]
        return ((values - mean) * lax.rsqrt(square - mean * mean + 1e-06) * gain).astype(
            jnp.bfloat16
        )

    for head in range(width // HEAD):
        queries = unit(total(q_ref, 0, head), qg_ref, head)
        keys = unit(total(k_ref, 1, head), kg_ref, head)
        values = total(v_ref, 2, head).astype(jnp.bfloat16)
        scores = lax.dot_general(
            queries, keys, (((1,), (1,)), ((), ())), preferred_element_type=jnp.float32
        ) * (HEAD**-0.5)
        expd = jnp.exp(scores - jnp.max(scores, axis=1, keepdims=True))
        probs = (expd / jnp.sum(expd, axis=1, keepdims=True)).astype(jnp.bfloat16)
        out_ref[:, head * HEAD : (head + 1) * HEAD] = jnp.dot(
            probs, values, preferred_element_type=jnp.float32
        ).astype(jnp.bfloat16)


def attend(query, key, value, other, query_gain, key_gain):
    rows, width = query.shape[0], query.shape[1] // 2

    def block(columns):
        return pl.BlockSpec((PATCHES, columns), lambda i: (i, 0))

    gain_spec = pl.BlockSpec((1, query_gain.shape[0]), lambda i: (0, 0))
    heads = rows // PATCHES * (width // HEAD)
    return pl.pallas_call(
        attend_kernel,
        grid=(rows // PATCHES,),
        out_shape=jax.ShapeDtypeStruct((rows, width), jnp.bfloat16),
        in_specs=[block(2 * width)] * 3 + [block(3 * width)] + [gain_spec] * 2,
        out_specs=block(width),
        compiler_params=pltpu.CompilerParams(vmem_limit_bytes=24 * 1024 * 1024),
        cost_estimate=pl.CostEstimate(
            flops=heads * PATCHES * PATCHES * HEAD * 4,
            bytes_accessed=rows * width * (12 + 12 + 6 + 2),
            transcendentals=heads * PATCHES * PATCHES,
        ),
    )(query, key, value, other, query_gain[None, :], key_gain[None, :])


def ringed(
    tokens, ln_gain, w_query, w_key, w_value, w_in, query_gain, key_gain, w_attn_out, w_mlp_out
):
    n_hid, n_wid = lax.axis_size("hid"), lax.axis_size("wid")
    hid = lax.axis_index("hid")
    core, side = hid % 2, hid // 2
    width = tokens.shape[1] * n_hid
    tokens_f = tokens.astype(jnp.float32)
    sums = jnp.stack([jnp.sum(tokens_f, axis=1), jnp.sum(tokens_f * tokens_f, axis=1)])
    sums = sums + swap(sums, 1)
    sums = sums + swap(sums, 2)
    mean = sums[0][:, None] / width
    square = sums[1][:, None] / width
    block = (
        (tokens_f - mean) * lax.rsqrt(square - mean * mean + 1e-06) * ln_gain.astype(jnp.float32)
    ).astype(jnp.bfloat16)
    blocks = [block]
    for _ in range(n_wid - 1):
        blocks.append(onward(blocks[-1]))

    def project(block):
        query, key, value, pre = [
            jnp.dot(block, weight, preferred_element_type=jnp.float32)
            for weight in (w_query, w_key, w_value, w_in)
        ]
        (paired,), other = reduce_columns([pre], core, side, jnp.bfloat16, jnp.bfloat16)
        pre = half(paired, side) + other.astype(jnp.float32)
        act = jax.nn.gelu(pre, approximate=False).astype(jnp.bfloat16)
        act = gather_columns(act, core, side)
        heads, other = reduce_columns(
            [query, key, value], core, side, jnp.float32, jnp.bfloat16
        )
        attended = attend(*heads, other, query_gain, key_gain)
        return act, gather_columns(attended, core, side)

    running = None
    ahead = [project(blocks[0])]
    for step in range(n_wid):
        if step + 1 < n_wid:
            block = blocks[step + 1]
            if step > 0:
                block, _ = lax.optimization_barrier((block, total))
            ahead.append(project(block))
        act, attended = ahead[step]
        total = jnp.dot(act, w_mlp_out, preferred_element_type=jnp.float32)
        total = total + jnp.dot(attended, w_attn_out, preferred_element_type=jnp.float32)
        summed = total if running is None else total + running.astype(jnp.float32)
        running = onward(summed.astype(jnp.bfloat16))
    return (tokens_f + running.astype(jnp.float32)).astype(jnp.bfloat16)


def choose(*args):
    if fast_fits(args[0], args[2]):
        return ringed(*args)
    return per_device(*args)


def solution(mesh):
    in_specs = (
        P(("groups", "wid"), "hid"),
        P("hid"),
        P("hid", "wid"),
        P("hid", "wid"),
        P("hid", "wid"),
        P("hid", "wid"),
        P("wid"),
        P("wid"),
        P("wid", "hid"),
        P("wid", "hid"),
    )
    out_specs = P(("groups", "wid"), "hid")
    return jax.shard_map(
        choose, mesh=mesh, in_specs=in_specs, out_specs=out_specs, check_vma=False
    )
```
